32 devices in a mesh: section: 4 (over y, core), kv: 4 (over z), tp: 2 (over x).
Axes of the slice: x: 2, y: 2, z: 4, core: 2. Of those that a mesh axis runs over, the one named last changes fastest.
Arguments:
- patches: bfloat16 [32768, 1152], P(('section', 'kv'), 'tp'), may hold values from -6 to 6
- vis_gain: float32 [1152], replicated, may hold values from 0.1 to 1.9
- vis_bias: float32 [1152], replicated, may hold values from -3 to 3
- w_proj: bfloat16 [1152, 4608], P('section', 'tp')
- b_proj: float32 [4608], P('tp'), may hold values from -12 to 12
- rms_gain: float32 [4608], P('tp'), may hold values from 0.1 to 1.9
- w_kv: bfloat16 [4608, 2, 1024], P('tp'), may hold values from -0.09375 to 0.09375
- queries: bfloat16 [16, 2048], P('section', 'tp'), may hold values from -18 to 18
- cache: bfloat16 [256, 128, 2, 1024], P(('section', 'kv'), None, None, 'tp'), may hold values from -6 to 6
- cache_lengths: int32 [4, 4], P('section'), may hold values from 1 to 7296, 7680 in all within a row
- slot_page: int32 [4, 64], P('section', 'kv'), may hold values from 0 to 63, each once within a row
- page_owner: int32 [4, 64], replicated, may hold values from 0 to 3, as said below
- image_request: int32 [4, 2], P('section'), may hold values from 0 to 3
Outputs:
- new_pages: bfloat16 [512, 128, 2, 1024], P(('section', 'kv'), None, None, 'tp')
- attended: bfloat16 [16, 2048], P('section', 'tp')
The draws below stay inside these ranges and needn't reach their ends.
Inputs may be any that keep to these rules, and one draw needn't show every extreme that they name: `page_owner`: from each source's 16 pages at most 8 go to any one owner; in every group one owner receives exactly 8 pages from every source.
All inputs are finite; a program needn't handle non-finite values.
Results may differ from the reference program's by a relative error of at most 0.0063.
Values may be sent and summed in bfloat16 or wider, within the bound.
A program may use at most 128 MiB of HBM per device.

```python
import math
import jax
import jax.numpy as jnp
import numpy as np
from jax import lax

D_VIS = 1152
D = 4608
HEAD_DIM = 128
KV_HEADS = 8
Q_HEADS = 16
PAGE = 128
IMAGE_PAGES = 32
IMG_GRP = 2
REQ_GRP = 4
KVW = 1024
QW = 2048
PAGES_DEV = 16
ROWS_DEV = 2048
PATCHES = 32768
CAP = 8
RECV = 32
SLOTS_GRP = 64
TOK_GRP = 7680
MAX_LEN = 7296
REQUESTS = 16
N_SECTION = 4
N_KV = 4


def draw_w_proj(key, part):
    column = jnp.arange(D, dtype=jnp.float32) / D
    spread_key = jax.random.fold_in(key, 11)
    entry_key = jax.random.fold_in(key, 12)
    spread = jax.random.uniform(spread_key, (D,), jnp.float32)
    entries = jax.random.normal(entry_key, (D_VIS, D), jnp.float32)
    scales = 10.0 ** (0.5 * column + 0.5 * spread)
    return (entries * scales[None, :] * D_VIS ** (-0.5)).astype(jnp.bfloat16)


def draw_page_owner(key, part):

    def one_group(group_key):
        hottest = jax.random.randint(jax.random.fold_in(group_key, 1), (), 0, N_KV)

        def one_block(block_key):
            shuffled = jax.random.permutation(jax.random.fold_in(block_key, 2), N_KV - 1)
            others = shuffled + (shuffled >= hottest).astype(jnp.int32)
            offset = jax.random.randint(jax.random.fold_in(block_key, 3), (), 0, 2)
            position = jnp.arange(PAGES_DEV, dtype=jnp.int32)
            index = jnp.clip((position - CAP + offset) // CAP, 0, max(N_KV - 2, 0))
            owners = jnp.where(position < CAP, hottest, others[index])
            order = jax.random.permutation(jax.random.fold_in(block_key, 4), PAGES_DEV)
            return owners[order]
        block_keys = jax.random.split(jax.random.fold_in(group_key, 5), N_KV)
        return jax.vmap(one_block)(block_keys).reshape(-1)
    group_keys = jax.random.split(jax.random.fold_in(key, 21), N_SECTION)
    return jax.vmap(one_group)(group_keys).astype(jnp.int32)


def plant(result, rng, least, largest):
    spot = [jax.random.randint(jax.random.fold_in(rng, axis), (), 0, length) for axis, length in enumerate(result.shape)]
    longest = result.shape.index(max(result.shape))
    next_to = spot[:longest] + [(spot[longest] + 1) % result.shape[longest]] + spot[longest + 1:]
    return result.at[tuple(spot)].set(least).at[tuple(next_to)].set(largest)


def shard_levels(rng, dims, shards, low, largest):
    def one(dim, parts):
        steps = jax.random.uniform(jax.random.fold_in(jax.random.fold_in(rng, 6), dim), (parts,), jnp.float32, low / len(shards), largest / len(shards))
        return jnp.repeat(jnp.exp(steps), dims[dim] // parts).reshape((-1,) + (1,) * (len(dims) - dim - 1))

    level = one(*shards[0])
    for cut in shards[1:]:
        level = level * one(*cut)
    return level


def profile(number_of, total, limit, lean):
    portions = [(1 << 20) // math.isqrt(grade ** lean) + 1 for grade in range(2, number_of + 1)]
    spare, counts = total - limit - (number_of - 1), [1] * (number_of - 1)
    while spare > 0:
        free = [i for i in range(number_of - 1) if counts[i] < limit]
        mass, left = sum([portions[i] for i in free]), spare
        for i in free:
            addition = min(limit - counts[i], max(1, left * portions[i] // mass), spare)
            counts[i] = counts[i] + addition
            spare = spare - addition
    return np.array([limit] + counts)


def ragged_sizes(rng, number_of, total, reach, skew):
    if number_of == 2:
        one = jax.random.randint(rng, (), max(1, total - reach), min(reach, total - 1) + 1)
        return jnp.stack([one, total - one])
    tallies = jnp.asarray(profile(number_of, total, reach, skew), jnp.int32)
    twos = (number_of - 1) // 2
    source_of, receiver = tallies[1:1 + 2 * twos:2], tallies[2:2 + 2 * twos:2]
    room = jnp.minimum(source_of - 1, reach - receiver)
    moved = jax.random.randint(jax.random.fold_in(rng, 1), (twos,), 0, 1 << 20) % (room + 1)
    tallies = tallies.at[1:1 + 2 * twos:2].set(source_of - moved).at[2:2 + 2 * twos:2].set(receiver + moved)
    return tallies[jax.random.permutation(jax.random.fold_in(rng, 2), number_of)]


def scatter_about(stream_key, dims, width, reach, cuts=(), held_as=jnp.bfloat16):
    factor_of = shard_levels(stream_key, dims, cuts, -0.22, 0.18) if cuts else 1.0
    drawn = jax.random.normal(stream_key, dims, jnp.float32) * width * factor_of
    return jnp.minimum(jnp.maximum(drawn, -reach), reach).astype(held_as)


def setup_inputs(seed: int = 0) -> dict:
    streams_of = jax.random.split(jax.random.key(seed), 14)
    patches = scatter_about(streams_of[0], (PATCHES, D_VIS), 1.0, 6.0, ((0, 16), (1, 2)))
    vis_gain = jnp.clip(1.0 + 0.18 * jax.random.normal(streams_of[1], (D_VIS,), jnp.float32), 0.1, 1.9)
    vis_bias = scatter_about(streams_of[2], (D_VIS,), 0.5, 3.0, (), jnp.float32)
    w_proj = draw_w_proj(jax.random.fold_in(streams_of[13], 71), 0)
    b_proj = scatter_about(streams_of[4], (D,), 2.0, 12.0, ((0, 2),), jnp.float32)
    rms_gain = jnp.clip(1.0 + 0.18 * jax.random.normal(streams_of[5], (D,), jnp.float32), 0.1, 1.9)
    w_kv = scatter_about(streams_of[6], (D, 2, KVW), D ** -0.5, 0.09375, ((0, 2),))
    queries = scatter_about(streams_of[7], (REQUESTS, QW), 3.0, 18.0, ((0, 4), (1, 2)))
    cache = scatter_about(streams_of[8], (N_SECTION * SLOTS_GRP, PAGE, 2, KVW), 1.0, 6.0, ((0, 16), (3, 2)))
    cache_lengths = jax.vmap(lambda own: ragged_sizes(own, REQ_GRP, TOK_GRP, MAX_LEN, 2))(jax.random.split(streams_of[9], N_SECTION)).reshape((N_SECTION, REQ_GRP)).astype(jnp.int32)
    slot_page = jax.vmap(lambda own: jax.random.permutation(own, SLOTS_GRP))(jax.random.split(streams_of[10], N_SECTION)).reshape((N_SECTION, SLOTS_GRP)).astype(jnp.int32)
    page_owner = draw_page_owner(jax.random.fold_in(streams_of[13], 71), 0)
    image_request = plant(jax.random.randint(streams_of[12], (N_SECTION, IMG_GRP), 0, REQ_GRP), jax.random.fold_in(streams_of[12], 1), 0, REQ_GRP - 1).astype(jnp.int32)
    return dict(patches=patches, vis_gain=vis_gain, vis_bias=vis_bias, w_proj=w_proj, b_proj=b_proj, rms_gain=rms_gain, w_kv=w_kv, queries=queries, cache=cache, cache_lengths=cache_lengths, slot_page=slot_page, page_owner=page_owner, image_request=image_request)


query_scale = 1.0 / 12.0
softcap = 50.0
epsilon = 1e-06

def block_ranks(owners):
    per_block = owners.shape[1]
    same_owner = owners[:, :, None] == owners[:, None, :]
    earlier = jnp.arange(per_block)[None, :] < jnp.arange(per_block)[:, None]
    return lax.optimization_barrier(jnp.sum((same_owner & earlier[None, :, :]).astype(jnp.int32), axis=2))

def encode_group(patch_rows, vis_gain, vis_bias, w_proj, b_proj, rms_gain, w_flat):
    values_in = patch_rows.astype(jnp.float32)
    row_mean = lax.optimization_barrier(jnp.mean(values_in, axis=1, keepdims=True))
    centred = values_in - row_mean
    variance = lax.optimization_barrier(jnp.mean(centred * centred, axis=1, keepdims=True))
    x_norm = (centred * lax.rsqrt(variance + epsilon) * vis_gain + vis_bias).astype(jnp.bfloat16)
    projected = jnp.dot(x_norm, w_proj, preferred_element_type=jnp.float32) + b_proj
    mean_square = lax.optimization_barrier(jnp.mean(projected * projected, axis=1, keepdims=True))
    hidden = (projected * lax.rsqrt(mean_square + epsilon) * rms_gain).astype(jnp.bfloat16)
    return jnp.dot(hidden, w_flat, preferred_element_type=jnp.float32).astype(jnp.bfloat16)

def place_group(pages_group, owners_row):
    owners = owners_row.reshape(N_KV, PAGES_DEV).astype(jnp.int32)
    ranks_grid = block_ranks(owners)
    source = jnp.arange(N_KV, dtype=jnp.int32)[:, None]
    destination = (owners * RECV + source * CAP + ranks_grid).reshape(-1).astype(jnp.int32)
    buffer_zero = jnp.zeros((N_KV * RECV, PAGE, 2, KVW), jnp.bfloat16)
    return buffer_zero.at[destination].set(pages_group)

def attend_group(query_rows, cache_rows, lengths, slot_ids, image_pages, request_row):
    query_grid = query_rows.astype(jnp.float32).reshape(REQ_GRP, KV_HEADS, Q_HEADS // KV_HEADS, HEAD_DIM)
    page_counts = (lengths + PAGE - 1) // PAGE
    starts = jnp.cumsum(page_counts) - page_counts
    within = slot_ids[:, None] - starts[None, :]
    inside = (within >= 0) & (within < page_counts[None, :])
    valid = jnp.where(inside, jnp.clip(lengths[None, :] - within * PAGE, 0, PAGE), 0)
    cache_mask = (jnp.arange(PAGE)[None, :, None] < valid[:, None, :]).reshape(SLOTS_GRP * PAGE, REQ_GRP)
    page_image = jnp.arange(N_KV * PAGES_DEV, dtype=jnp.int32) // IMAGE_PAGES
    page_request = request_row[page_image]
    image_mask = jnp.repeat(page_request[:, None] == jnp.arange(REQ_GRP)[None, :], PAGE, axis=0)
    store = jnp.concatenate([cache_rows, image_pages], axis=0)
    allowed = jnp.concatenate([cache_mask, image_mask], axis=0).T
    keys = store[:, :, 0, :].reshape(-1, KV_HEADS, HEAD_DIM).astype(jnp.float32)
    values = store[:, :, 1, :].reshape(-1, KV_HEADS, HEAD_DIM).astype(jnp.float32)
    raw_scores = jnp.einsum('rkgd,tkd->rkgt', query_grid, keys, precision=lax.Precision.HIGHEST)
    capped = softcap * jnp.tanh(raw_scores * query_scale / softcap)
    weights = jnp.where(allowed[:, None, None, :], jnp.exp(capped), jnp.float32(0.0))
    totals = lax.optimization_barrier(jnp.sum(weights, axis=3))
    rounded = lax.optimization_barrier(weights.astype(jnp.bfloat16)).astype(jnp.float32)
    weighted = jnp.einsum('rkgt,tkd->rkgd', rounded, values, precision=lax.Precision.HIGHEST)
    return (weighted / totals[..., None]).astype(jnp.bfloat16).reshape(REQ_GRP, QW)

def reference(patches, vis_gain, vis_bias, w_proj, b_proj, rms_gain, w_kv, queries, cache, cache_lengths, slot_page, page_owner, image_request):
    w_flat = w_kv.reshape(D, 2 * KVW)
    patch_groups = patches.reshape(N_SECTION, N_KV * ROWS_DEV, D_VIS)
    encoded = lax.map(lambda rows_in: encode_group(rows_in, vis_gain, vis_bias, w_proj, b_proj, rms_gain, w_flat), patch_groups)
    pages_all = encoded.reshape(N_SECTION, N_KV * PAGES_DEV, PAGE, 2, KVW)
    handed = jnp.roll(pages_all, 1, axis=0)
    placed = lax.map(lambda paired: place_group(paired[0], paired[1]), (handed, page_owner))
    new_pages = placed.reshape(N_SECTION * N_KV * RECV, PAGE, 2, KVW)
    group_inputs = (queries.reshape(N_SECTION, REQ_GRP, QW), cache.reshape(N_SECTION, SLOTS_GRP, PAGE, 2, KVW), cache_lengths, slot_page, handed, image_request)
    attended = lax.map(lambda group_in: attend_group(*group_in), group_inputs).reshape(REQUESTS, QW)
    return (new_pages, attended)
```

```python
import jax
import jax.numpy as jnp
from jax import lax
from jax.sharding import PartitionSpec as P

HEAD_DIM = 128
IMAGE_PAGES = 32


query_scale = 1.0 / 12.0
softcap = 50.0
epsilon = 1e-06


CHUNKS = 4


def from_behind(value, axis, steps):
    count = lax.axis_size(axis)
    pairs = [(source, (source + steps) % count) for source in range(count)]
    return lax.ppermute(value, axis, pairs)


def gather_features(block):
    if lax.axis_size("tp") != 2:
        return lax.all_gather(block, "tp", axis=1, tiled=True)
    other = from_behind(block, "tp", 1)
    first = lax.axis_index("tp") == 0
    return jnp.concatenate(
        [jnp.where(first, block, other), jnp.where(first, other, block)], axis=1
    )


def sum_over_tp(value):
    if lax.axis_size("tp") != 2:
        return lax.psum(value, "tp")
    return value + from_behind(value, "tp", 1)


def columns_of(w_kv, member):
    width = w_kv.shape[2] // lax.axis_size("tp")
    part = lax.dynamic_slice_in_dim(w_kv, member * width, width, axis=2)
    return part.reshape(w_kv.shape[0], 2 * width)


def block_ranks(owners):
    per_block = owners.shape[1]
    same_owner = owners[:, :, None] == owners[:, None, :]
    earlier = jnp.arange(per_block)[None, :] < jnp.arange(per_block)[:, None]
    return jnp.sum((same_owner & earlier[None, :, :]).astype(jnp.int32), axis=2)


def attend_part(query_grid, page_store, token_mask):
    slot_count = page_store.shape[0]
    page_len = page_store.shape[1]
    head_count = page_store.shape[3] // HEAD_DIM
    keys = page_store[:, :, 0, :].reshape(slot_count * page_len, head_count, HEAD_DIM)
    values = page_store[:, :, 1, :].reshape(slot_count * page_len, head_count, HEAD_DIM)
    raw_scores = jnp.einsum("rkgd,tkd->rkgt", query_grid, keys, preferred_element_type=jnp.float32)
    capped = softcap * jnp.tanh(raw_scores * query_scale / softcap)
    allowed = token_mask.reshape(slot_count * page_len, -1).T
    weights = jnp.where(allowed[:, None, None, :], jnp.exp(capped), jnp.float32(0.0))
    totals = jnp.sum(weights, axis=3)
    weighted = jnp.einsum(
        "rkgt,tkd->rkgd", weights.astype(jnp.bfloat16), values, preferred_element_type=jnp.float32
    )
    return (totals, weighted)


def per_device(
    patches,
    vis_gain,
    vis_bias,
    w_proj,
    b_proj,
    rms_gain,
    w_kv,
    queries,
    cache,
    cache_lengths,
    slot_page,
    page_owner,
    image_request,
):
    kv_count = lax.axis_size("kv")
    section_count = lax.axis_size("section")
    section_idx = lax.axis_index("section")
    kv_idx = lax.axis_index("kv")
    row_count = patches.shape[0]
    page_len = cache.shape[1]
    pages_dev = row_count // page_len
    capacity = max(2, (2 * pages_dev + kv_count - 1) // kv_count)
    recv_slots = kv_count * capacity
    tp_count = lax.axis_size("tp")
    tp_idx = lax.axis_index("tp")
    full_w = lax.all_gather(w_proj, "section", axis=0, tiled=True)
    full_width = w_proj.shape[1] * tp_count
    w_parts = [columns_of(w_kv, (tp_idx + j) % tp_count) for j in range(tp_count)]
    tokens = page_len // CHUNKS
    patch_pages = patches.reshape(pages_dev, page_len, -1)
    own_owners = lax.dynamic_index_in_dim(page_owner, section_idx, 0, keepdims=False).reshape(
        kv_count, pages_dev
    )
    my_owner = lax.dynamic_index_in_dim(own_owners, kv_idx, 0, keepdims=False)
    my_rank = lax.dynamic_index_in_dim(block_ranks(own_owners), kv_idx, 0, keepdims=False)
    new_pages = jnp.zeros((recv_slots, page_len, 2, cache.shape[3]), jnp.bfloat16)
    handed_parts = []
    for c in range(CHUNKS):
        block = patch_pages[:, c * tokens : (c + 1) * tokens, :].reshape(pages_dev * tokens, -1)
        gathered = gather_features(block).astype(jnp.float32)
        row_mean = jnp.mean(gathered, axis=1, keepdims=True)
        centred = gathered - row_mean
        variance = jnp.mean(centred * centred, axis=1, keepdims=True)
        x_norm = (centred * lax.rsqrt(variance + epsilon) * vis_gain + vis_bias).astype(
            jnp.bfloat16
        )
        projected = jnp.dot(x_norm, full_w, preferred_element_type=jnp.float32) + b_proj
        squares = sum_over_tp(jnp.sum(projected * projected, axis=1))
        hidden = (
            projected * lax.rsqrt(squares / full_width + epsilon)[:, None] * rms_gain
        ).astype(jnp.bfloat16)
        arrived = [
            from_behind(
                jnp.dot(hidden, w_parts[j], preferred_element_type=jnp.float32).astype(
                    jnp.bfloat16
                ),
                "tp",
                j,
            )
            for j in range(1, tp_count)
        ]
        image_kv = jnp.dot(hidden, w_parts[0], preferred_element_type=jnp.float32)
        for part in arrived:
            image_kv = image_kv + part.astype(jnp.float32)
        handed = from_behind(
            image_kv.astype(jnp.bfloat16).reshape(pages_dev, tokens, -1), "section", 1
        )
        handed_parts.append(handed)
        for j in range(kv_count):
            owner = (kv_idx + j) % kv_count
            placing = (
                (jnp.arange(capacity)[:, None] == my_rank[None, :]) & (my_owner == owner)[None, :]
            ).astype(jnp.bfloat16)
            outgoing = jnp.einsum(
                "jp,ptf->jtf", placing, handed, preferred_element_type=jnp.float32
            ).astype(jnp.bfloat16)
            incoming = from_behind(outgoing, "kv", j) if j else outgoing
            source = (kv_idx - j) % kv_count
            new_pages = lax.dynamic_update_slice(
                new_pages,
                incoming.reshape(capacity, tokens, 2, -1),
                (source * capacity, c * tokens, 0, 0),
            )
    req_count = queries.shape[0]
    kv_heads_dev = cache.shape[3] // HEAD_DIM
    group_size = queries.shape[1] // HEAD_DIM // kv_heads_dev
    query_grid = queries.reshape(req_count, kv_heads_dev, group_size, HEAD_DIM)
    lengths = cache_lengths[0]
    page_counts = (lengths + page_len - 1) // page_len
    starts = jnp.cumsum(page_counts) - page_counts
    slot_ids = slot_page[0]
    within = slot_ids[:, None] - starts[None, :]
    inside = (within >= 0) & (within < page_counts[None, :])
    valid = jnp.where(inside, jnp.clip(lengths[None, :] - within * page_len, 0, page_len), 0)
    cache_mask = jnp.arange(page_len)[None, :, None] < valid[:, None, :]
    cache_totals, cache_weighted = attend_part(query_grid, cache, cache_mask)
    image_of = (kv_idx * pages_dev + jnp.arange(pages_dev)) // IMAGE_PAGES
    image_hit = image_of[:, None] == jnp.arange(image_request.shape[1])[None, :]
    page_request = jnp.sum(jnp.where(image_hit, image_request[0][None, :], 0), axis=1)
    request_hit = page_request[:, None] == jnp.arange(req_count)[None, :]
    handed_mask = jnp.broadcast_to(request_hit[:, None, :], (pages_dev, tokens, req_count))
    totals, weighted = cache_totals, cache_weighted
    for handed in handed_parts:
        part_totals, part_weighted = attend_part(
            query_grid, handed.reshape(pages_dev, tokens, 2, -1), handed_mask
        )
        totals, weighted = totals + part_totals, weighted + part_weighted
    totals, weighted = lax.psum((totals, weighted), "kv")
    attended = (weighted / totals[..., None]).astype(jnp.bfloat16).reshape(req_count, -1)
    return (new_pages, attended)


def solution(mesh):
    in_specs = (
        P(("section", "kv"), "tp"),
        P(),
        P(),
        P("section", "tp"),
        P("tp"),
        P("tp"),
        P("tp", None, None),
        P("section", "tp"),
        P(("section", "kv"), None, None, "tp"),
        P("section", None),
        P("section", "kv"),
        P(),
        P("section", None),
    )
    out_specs = (P(("section", "kv"), None, None, "tp"), P("section", "tp"))
    return jax.shard_map(
        per_device, mesh=mesh, in_specs=in_specs, out_specs=out_specs, check_vma=False
    )
```

```python
import jax
import jax.numpy as jnp
from jax import lax
from jax.experimental import pallas as pl
from jax.experimental.pallas import tpu as pltpu
from jax.sharding import PartitionSpec as P

HEAD_DIM = 128
IMAGE_PAGES = 32


query_scale = 1.0 / 12.0
softcap = 50.0
epsilon = 1e-06


CHUNKS = 4


def from_behind(value, axis, steps):
    count = lax.axis_size(axis)
    pairs = [(source, (source + steps) % count) for source in range(count)]
    return lax.ppermute(value, axis, pairs)


def gather_features(block):
    if lax.axis_size("tp") != 2:
        return lax.all_gather(block, "tp", axis=1, tiled=True)
    other = from_behind(block, "tp", 1)
    first = lax.axis_index("tp") == 0
    return jnp.concatenate(
        [jnp.where(first, block, other), jnp.where(first, other, block)], axis=1
    )


def sum_over_tp(value):
    if lax.axis_size("tp") != 2:
        return lax.psum(value, "tp")
    return value + from_behind(value, "tp", 1)


def columns_of(w_kv, member):
    width = w_kv.shape[2] // lax.axis_size("tp")
    part = lax.dynamic_slice_in_dim(w_kv, member * width, width, axis=2)
    return part.reshape(w_kv.shape[0], 2 * width)


def block_ranks(owners):
    per_block = owners.shape[1]
    same_owner = owners[:, :, None] == owners[:, None, :]
    earlier = jnp.arange(per_block)[None, :] < jnp.arange(per_block)[:, None]
    return jnp.sum((same_owner & earlier[None, :, :]).astype(jnp.int32), axis=2)


def attend_kernel(head_count, parts, query_ref, *refs):
    masks, stores = refs[:parts], refs[parts : 2 * parts]
    totals_ref, weighted_ref = refs[2 * parts :]
    half = head_count * HEAD_DIM
    for k in range(head_count):
        query = query_ref[k]
        total = jnp.zeros((query.shape[0], 1), jnp.float32)
        numer = jnp.zeros((query.shape[0], HEAD_DIM), jnp.float32)
        for mask_ref, store_ref in zip(masks, stores):
            keys = store_ref[:, k * HEAD_DIM : (k + 1) * HEAD_DIM]
            values = store_ref[:, half + k * HEAD_DIM : half + (k + 1) * HEAD_DIM]
            raw = lax.dot_general(
                query, keys, (((1,), (1,)), ((), ())), preferred_element_type=jnp.float32
            )
            capped = softcap * jnp.tanh(raw * query_scale / softcap)
            weights = jnp.where(mask_ref[...] > 0.0, jnp.exp(capped), jnp.float32(0.0))
            total = total + jnp.sum(weights, axis=1, keepdims=True)
            numer = numer + jnp.dot(
                weights.astype(jnp.bfloat16), values, preferred_element_type=jnp.float32
            )
        totals_ref[k] = jnp.broadcast_to(total, numer.shape)
        weighted_ref[k] = numer


def attend_all(query_grid, masks, stores):
    head_count, rows = query_grid.shape[:2]
    tokens = sum(store.shape[0] for store in stores)
    result = jax.ShapeDtypeStruct((head_count, rows, HEAD_DIM), jnp.float32)
    return pl.pallas_call(
        lambda *refs: attend_kernel(head_count, len(stores), *refs),
        out_shape=(result, result),
        in_specs=[pl.BlockSpec(memory_space=pltpu.VMEM)] * (1 + 2 * len(stores)),
        out_specs=(pl.BlockSpec(memory_space=pltpu.VMEM),) * 2,
        compiler_params=pltpu.CompilerParams(vmem_limit_bytes=40 * 1024 * 1024),
        cost_estimate=pl.CostEstimate(
            flops=4 * tokens * head_count * rows * HEAD_DIM * 8,
            bytes_accessed=4 * tokens * head_count * HEAD_DIM,
            transcendentals=2 * tokens * head_count * rows,
        ),
    )(query_grid, *masks, *stores)


def sum_over_kv(value):
    count = lax.axis_size("kv")
    if count > 4:
        return lax.psum(value, "kv")
    here = lax.axis_index("kv")
    shifted = jnp.stack([from_behind(value, "kv", j) if j else value for j in range(count)])
    total = jnp.zeros_like(value)
    for source in range(count):
        total = total + lax.dynamic_index_in_dim(
            shifted, (here - source + count) % count, 0, keepdims=False
        )
    return total


def per_device(
    patches,
    vis_gain,
    vis_bias,
    w_proj,
    b_proj,
    rms_gain,
    w_kv,
    queries,
    cache,
    cache_lengths,
    slot_page,
    page_owner,
    image_request,
):
    kv_count = lax.axis_size("kv")
    section_count = lax.axis_size("section")
    section_idx = lax.axis_index("section")
    kv_idx = lax.axis_index("kv")
    row_count = patches.shape[0]
    page_len = cache.shape[1]
    pages_dev = row_count // page_len
    capacity = max(2, (2 * pages_dev + kv_count - 1) // kv_count)
    recv_slots = kv_count * capacity
    tp_count = lax.axis_size("tp")
    tp_idx = lax.axis_index("tp")
    full_w = lax.all_gather(w_proj, "section", axis=0, tiled=True)
    full_width = w_proj.shape[1] * tp_count
    w_parts = [columns_of(w_kv, (tp_idx + j) % tp_count) for j in range(tp_count)]
    tokens = page_len // CHUNKS
    patch_pages = patches.reshape(pages_dev, page_len, -1)
    own_owners = lax.dynamic_index_in_dim(page_owner, section_idx, 0, keepdims=False).reshape(
        kv_count, pages_dev
    )
    my_owner = lax.dynamic_index_in_dim(own_owners, kv_idx, 0, keepdims=False)
    my_rank = lax.dynamic_index_in_dim(block_ranks(own_owners), kv_idx, 0, keepdims=False)
    new_pages = jnp.zeros((recv_slots, page_len, 2, cache.shape[3]), jnp.bfloat16)
    handed_parts = []
    outgoing_all = []

    def exchange(pages, blocks, c):
        for j in range(kv_count):
            incoming = from_behind(blocks[j], "kv", j) if j else blocks[j]
            source = (kv_idx - j + kv_count) % kv_count
            pages = lax.dynamic_update_slice(
                pages,
                incoming.reshape(capacity, tokens, 2, -1),
                (source * capacity, c * tokens, 0, 0),
            )
        return pages

    for c in range(CHUNKS):
        block = patch_pages[:, c * tokens : (c + 1) * tokens, :].reshape(pages_dev * tokens, -1)
        gathered = gather_features(block).astype(jnp.float32)
        row_mean = jnp.mean(gathered, axis=1, keepdims=True)
        centred = gathered - row_mean
        variance = jnp.mean(centred * centred, axis=1, keepdims=True)
        x_norm = (centred * lax.rsqrt(variance + epsilon) * vis_gain + vis_bias).astype(
            jnp.bfloat16
        )
        projected = jnp.dot(x_norm, full_w, preferred_element_type=jnp.float32) + b_proj
        squares = sum_over_tp(jnp.sum(projected * projected, axis=1))
        hidden = (
            projected * lax.rsqrt(squares / full_width + epsilon)[:, None] * rms_gain
        ).astype(jnp.bfloat16)
        arrived = [
            from_behind(
                jnp.dot(hidden, w_parts[j], preferred_element_type=jnp.float32).astype(
                    jnp.bfloat16
                ),
                "tp",
                j,
            )
            for j in range(1, tp_count)
        ]
        if outgoing_all:
            hidden, *outgoing_all = lax.optimization_barrier((hidden, *outgoing_all))
            new_pages = exchange(new_pages, outgoing_all, c - 1)
        image_kv = jnp.dot(hidden, w_parts[0], preferred_element_type=jnp.float32)
        for part in arrived:
            image_kv = image_kv + part.astype(jnp.float32)
        handed = from_behind(
            image_kv.astype(jnp.bfloat16).reshape(pages_dev, tokens, -1), "section", 1
        )
        handed_parts.append(handed)
        outgoing_all = []
        for j in range(kv_count):
            owner = (kv_idx + j) % kv_count
            placing = (
                (jnp.arange(capacity)[:, None] == my_rank[None, :]) & (my_owner == owner)[None, :]
            ).astype(jnp.bfloat16)
            outgoing = jnp.einsum(
                "jp,ptf->jtf", placing, handed, preferred_element_type=jnp.float32
            ).astype(jnp.bfloat16)
            outgoing_all.append(outgoing)
    cache, queries, *outgoing_all = lax.optimization_barrier((cache, queries, *outgoing_all))
    new_pages = exchange(new_pages, outgoing_all, CHUNKS - 1)
    req_count = queries.shape[0]
    kv_heads_dev = cache.shape[3] // HEAD_DIM
    group_size = queries.shape[1] // HEAD_DIM // kv_heads_dev
    query_grid = (
        queries.reshape(req_count, kv_heads_dev, group_size, HEAD_DIM)
        .transpose(1, 0, 2, 3)
        .reshape(kv_heads_dev, req_count * group_size, HEAD_DIM)
    )
    lengths = cache_lengths[0]
    page_counts = (lengths + page_len - 1) // page_len
    starts = jnp.cumsum(page_counts) - page_counts
    slot_ids = slot_page[0]
    within = slot_ids[:, None] - starts[None, :]
    inside = (within >= 0) & (within < page_counts[None, :])
    valid = jnp.where(inside, jnp.clip(lengths[None, :] - within * page_len, 0, page_len), 0)
    cache_mask = jnp.arange(page_len)[None, :, None] < valid[:, None, :]
    image_of = (kv_idx * pages_dev + jnp.arange(pages_dev)) // IMAGE_PAGES
    image_hit = image_of[:, None] == jnp.arange(image_request.shape[1])[None, :]
    page_request = jnp.sum(jnp.where(image_hit, image_request[0][None, :], 0), axis=1)
    request_hit = page_request[:, None] == jnp.arange(req_count)[None, :]
    handed_mask = jnp.broadcast_to(request_hit[:, None, :], (pages_dev, tokens, req_count))

    def grouped(mask):
        rows = mask.reshape(-1, req_count).T.astype(jnp.float32)
        return jnp.repeat(rows, group_size, axis=0)

    totals, weighted = attend_all(
        query_grid,
        [grouped(cache_mask)] + [grouped(handed_mask)] * CHUNKS,
        [cache.reshape(-1, 2 * cache.shape[3])]
        + [handed.reshape(pages_dev * tokens, -1) for handed in handed_parts],
    )
    totals, weighted = sum_over_kv(jnp.stack([totals, weighted]))
    attended = (
        (weighted / totals)
        .astype(jnp.bfloat16)
        .reshape(kv_heads_dev, req_count, group_size, HEAD_DIM)
        .transpose(1, 0, 2, 3)
        .reshape(req_count, -1)
    )
    return (new_pages, attended)


def solution(mesh):
    in_specs = (
        P(("section", "kv"), "tp"),
        P(),
        P(),
        P("section", "tp"),
        P("tp"),
        P("tp"),
        P("tp", None, None),
        P("section", "tp"),
        P(("section", "kv"), None, None, "tp"),
        P("section", None),
        P("section", "kv"),
        P(),
        P("section", None),
    )
    out_specs = (P(("section", "kv"), None, None, "tp"), P("section", "tp"))
    return jax.shard_map(
        per_device, mesh=mesh, in_specs=in_specs, out_specs=out_specs, check_vma=False
    )
```

```python
import jax
import jax.numpy as jnp
from jax import lax
from jax.experimental import pallas as pl
from jax.experimental.pallas import tpu as pltpu
from jax.sharding import PartitionSpec as P

HEAD_DIM = 128
IMAGE_PAGES = 32


query_scale = 1.0 / 12.0
softcap = 50.0
epsilon = 1e-06


CHUNKS = 4


def from_behind(value, axis, steps):
    count = lax.axis_size(axis)
    pairs = [(source, (source + steps) % count) for source in range(count)]
    return lax.ppermute(value, axis, pairs)


def hand_over(value, steps):
    sections, count = lax.axis_size("section"), lax.axis_size("kv")
    pairs = [
        (s * count + k, ((s + 1) % sections) * count + (k + steps) % count)
        for s in range(sections)
        for k in range(count)
    ]
    return lax.ppermute(value, ("section", "kv"), pairs)


def after(value, *earlier):
    return lax.optimization_barrier((value, *earlier))[0]


def gather_features(block, earlier):
    if lax.axis_size("tp") != 2:
        return lax.all_gather(block, "tp", axis=1, tiled=True)
    other = from_behind(block, "tp", 1)
    if earlier is not None:
        other = after(other, earlier)
    first = lax.axis_index("tp") == 0
    return jnp.concatenate(
        [jnp.where(first, block, other), jnp.where(first, other, block)], axis=1
    )


def sum_over_tp(value):
    if lax.axis_size("tp") != 2:
        return lax.psum(value, "tp")
    return value + from_behind(value, "tp", 1)


def columns_of(w_kv, member):
    width = w_kv.shape[2] // lax.axis_size("tp")
    part = lax.dynamic_slice_in_dim(w_kv, member * width, width, axis=2)
    return part.reshape(w_kv.shape[0], 2 * width)


def block_ranks(owners):
    per_block = owners.shape[1]
    same_owner = owners[:, :, None] == owners[:, None, :]
    earlier = jnp.arange(per_block)[None, :] < jnp.arange(per_block)[:, None]
    return jnp.sum((same_owner & earlier[None, :, :]).astype(jnp.int32), axis=2)


def attend_kernel(head_count, parts, query_ref, *refs):
    masks, stores = refs[:parts], refs[parts : 2 * parts]
    totals_ref, weighted_ref = refs[2 * parts :]
    half = head_count * HEAD_DIM
    for k in range(head_count):
        query = query_ref[k]
        total = jnp.zeros((query.shape[0], 1), jnp.float32)
        numer = jnp.zeros((query.shape[0], HEAD_DIM), jnp.float32)
        for mask_ref, store_ref in zip(masks, stores):
            keys = store_ref[:, k * HEAD_DIM : (k + 1) * HEAD_DIM]
            values = store_ref[:, half + k * HEAD_DIM : half + (k + 1) * HEAD_DIM]
            raw = lax.dot_general(
                query, keys, (((1,), (1,)), ((), ())), preferred_element_type=jnp.float32
            )
            capped = softcap * jnp.tanh(raw * query_scale / softcap)
            weights = jnp.where(mask_ref[...] > 0.0, jnp.exp(capped), jnp.float32(0.0))
            total = total + jnp.sum(weights, axis=1, keepdims=True)
            numer = numer + jnp.dot(
                weights.astype(jnp.bfloat16), values, preferred_element_type=jnp.float32
            )
        totals_ref[k] = jnp.broadcast_to(total, numer.shape)
        weighted_ref[k] = numer


def attend_all(query_grid, masks, stores):
    head_count, rows = query_grid.shape[:2]
    tokens = sum(store.shape[0] for store in stores)
    result = jax.ShapeDtypeStruct((head_count, rows, HEAD_DIM), jnp.float32)
    return pl.pallas_call(
        lambda *refs: attend_kernel(head_count, len(stores), *refs),
        out_shape=(result, result),
        in_specs=[pl.BlockSpec(memory_space=pltpu.VMEM)] * (1 + 2 * len(stores)),
        out_specs=(pl.BlockSpec(memory_space=pltpu.VMEM),) * 2,
        compiler_params=pltpu.CompilerParams(vmem_limit_bytes=40 * 1024 * 1024),
        cost_estimate=pl.CostEstimate(
            flops=4 * tokens * head_count * rows * HEAD_DIM * 8,
            bytes_accessed=4 * tokens * head_count * HEAD_DIM,
            transcendentals=2 * tokens * head_count * rows,
        ),
    )(query_grid, *masks, *stores)


def sum_over_kv(value):
    count = lax.axis_size("kv")
    if count > 4:
        return lax.psum(value, "kv")
    here = lax.axis_index("kv")
    shifted = jnp.stack([from_behind(value, "kv", j) if j else value for j in range(count)])
    total = jnp.zeros_like(value)
    for source in range(count):
        total = total + lax.dynamic_index_in_dim(
            shifted, (here - source + count) % count, 0, keepdims=False
        )
    return total


def per_device(
    patches,
    vis_gain,
    vis_bias,
    w_proj,
    b_proj,
    rms_gain,
    w_kv,
    queries,
    cache,
    cache_lengths,
    slot_page,
    page_owner,
    image_request,
):
    kv_count = lax.axis_size("kv")
    section_count = lax.axis_size("section")
    section_idx = lax.axis_index("section")
    kv_idx = lax.axis_index("kv")
    row_count = patches.shape[0]
    page_len = cache.shape[1]
    pages_dev = row_count // page_len
    capacity = max(2, (2 * pages_dev + kv_count - 1) // kv_count)
    recv_slots = kv_count * capacity
    tp_count = lax.axis_size("tp")
    tp_idx = lax.axis_index("tp")
    full_w = lax.all_gather(w_proj, "section", axis=0, tiled=True)
    full_width = w_proj.shape[1] * tp_count
    w_parts = [columns_of(w_kv, (tp_idx + j) % tp_count) for j in range(tp_count)]
    tokens = page_len // CHUNKS
    patch_pages = patches.reshape(pages_dev, page_len, -1)
    next_group = (section_idx + 1) % section_count
    next_owners = lax.dynamic_index_in_dim(page_owner, next_group, 0, keepdims=False).reshape(
        kv_count, pages_dev
    )
    my_owner = lax.dynamic_index_in_dim(next_owners, kv_idx, 0, keepdims=False)
    my_rank = lax.dynamic_index_in_dim(block_ranks(next_owners), kv_idx, 0, keepdims=False)
    new_pages = jnp.zeros((recv_slots, page_len, 2, cache.shape[3]), jnp.bfloat16)
    encoded_parts = []
    squares_before, encoded_before, marker = None, None, None
    shifts = list(range(1, kv_count)) + [0]
    waiting = []

    def write_pages(pages, blocks):
        for block, slot, token in blocks:
            pages = lax.dynamic_update_slice(
                pages, block.reshape(capacity, tokens, 2, -1), (slot, token, 0, 0)
            )
        return pages

    for c in range(CHUNKS):
        block = patch_pages[:, c * tokens : (c + 1) * tokens, :].reshape(pages_dev * tokens, -1)
        gathered = gather_features(block, squares_before).astype(jnp.float32)
        row_mean = jnp.mean(gathered, axis=1, keepdims=True)
        centred = gathered - row_mean
        variance = jnp.mean(centred * centred, axis=1, keepdims=True)
        x_norm = (centred * lax.rsqrt(variance + epsilon) * vis_gain + vis_bias).astype(
            jnp.bfloat16
        )
        projected = jnp.dot(x_norm, full_w, preferred_element_type=jnp.float32) + b_proj
        squares_before = jnp.sum(projected * projected, axis=1)
        squares = sum_over_tp(squares_before)
        hidden = (
            projected * lax.rsqrt(squares / full_width + epsilon)[:, None] * rms_gain
        ).astype(jnp.bfloat16)
        if encoded_before is not None:
            hidden = after(hidden, encoded_before)
        arrived = [
            from_behind(
                jnp.dot(hidden, w_parts[j], preferred_element_type=jnp.float32).astype(
                    jnp.bfloat16
                ),
                "tp",
                j,
            )
            for j in range(1, tp_count)
        ]
        if marker is not None:
            hidden = after(hidden, marker)
        image_kv = jnp.dot(hidden, w_parts[0], preferred_element_type=jnp.float32)
        for part in arrived:
            image_kv = image_kv + part.astype(jnp.float32)
        encoded = image_kv.astype(jnp.bfloat16).reshape(pages_dev, tokens, -1)
        encoded_before = encoded
        encoded_parts.append(encoded)
        for j in shifts:
            owner = (kv_idx + j) % kv_count
            placing = (
                (jnp.arange(capacity)[:, None] == my_rank[None, :]) & (my_owner == owner)[None, :]
            ).astype(jnp.bfloat16)
            outgoing = jnp.einsum(
                "jp,ptf->jtf", placing, encoded, preferred_element_type=jnp.float32
            ).astype(jnp.bfloat16)
            if j == shifts[0]:
                waiting = [(after(block, outgoing), *place) for block, *place in waiting]
                new_pages = write_pages(new_pages, waiting)
                waiting = []
            incoming = hand_over(outgoing, j)
            source = (kv_idx - j + kv_count) % kv_count
            if j == shifts[0]:
                marker = incoming
                new_pages = write_pages(new_pages, [(incoming, source * capacity, c * tokens)])
            else:
                waiting.append((incoming, source * capacity, c * tokens))
    next_queries = from_behind(queries, "section", section_count - 1)
    next_request = from_behind(image_request, "section", section_count - 1)
    cache = after(cache, marker)
    next_queries = after(next_queries, marker)
    req_count = queries.shape[0]
    kv_heads_dev = cache.shape[3] // HEAD_DIM
    group_size = queries.shape[1] // HEAD_DIM // kv_heads_dev

    def grid_of(rows):
        return (
            rows.reshape(req_count, kv_heads_dev, group_size, HEAD_DIM)
            .transpose(1, 0, 2, 3)
            .reshape(kv_heads_dev, req_count * group_size, HEAD_DIM)
        )

    lengths = cache_lengths[0]
    page_counts = (lengths + page_len - 1) // page_len
    starts = jnp.cumsum(page_counts) - page_counts
    slot_ids = slot_page[0]
    within = slot_ids[:, None] - starts[None, :]
    inside = (within >= 0) & (within < page_counts[None, :])
    valid = jnp.where(inside, jnp.clip(lengths[None, :] - within * page_len, 0, page_len), 0)
    cache_mask = jnp.arange(page_len)[None, :, None] < valid[:, None, :]
    image_of = (kv_idx * pages_dev + jnp.arange(pages_dev)) // IMAGE_PAGES
    image_hit = image_of[:, None] == jnp.arange(next_request.shape[1])[None, :]
    page_request = jnp.sum(jnp.where(image_hit, next_request[0][None, :], 0), axis=1)
    request_hit = page_request[:, None] == jnp.arange(req_count)[None, :]
    handed_mask = jnp.broadcast_to(request_hit[:, None, :], (pages_dev, tokens, req_count))

    def grouped(mask):
        rows = mask.reshape(-1, req_count).T.astype(jnp.float32)
        return jnp.repeat(rows, group_size, axis=0)

    image_sums = attend_all(
        grid_of(next_queries),
        [grouped(handed_mask)] * CHUNKS,
        [encoded.reshape(pages_dev * tokens, -1) for encoded in encoded_parts],
    )
    cache_sums = attend_all(
        grid_of(queries), [grouped(cache_mask)], [cache.reshape(-1, 2 * cache.shape[3])]
    )
    handed_sums = from_behind(jnp.stack(image_sums), "section", 1)
    local_sums = jnp.stack(cache_sums) + handed_sums
    waiting = [(after(block, local_sums), *place) for block, *place in waiting]
    new_pages = write_pages(new_pages, waiting)
    totals, weighted = sum_over_kv(local_sums)
    attended = (
        (weighted / totals)
        .astype(jnp.bfloat16)
        .reshape(kv_heads_dev, req_count, group_size, HEAD_DIM)
        .transpose(1, 0, 2, 3)
        .reshape(req_count, -1)
    )
    return (new_pages, attended)


def solution(mesh):
    in_specs = (
        P(("section", "kv"), "tp"),
        P(),
        P(),
        P("section", "tp"),
        P("tp"),
        P("tp"),
        P("tp", None, None),
        P("section", "tp"),
        P(("section", "kv"), None, None, "tp"),
        P("section", None),
        P("section", "kv"),
        P(),
        P("section", None),
    )
    out_specs = (P(("section", "kv"), None, None, "tp"), P("section", "tp"))
    return jax.shard_map(
        per_device, mesh=mesh, in_specs=in_specs, out_specs=out_specs, check_vma=False
    )
```

```python
import jax
import jax.numpy as jnp
from jax import lax
from jax.experimental import pallas as pl
from jax.experimental.pallas import tpu as pltpu
from jax.sharding import PartitionSpec as P

HEAD_DIM = 128
IMAGE_PAGES = 32


query_scale = 1.0 / 12.0
softcap = 50.0
epsilon = 1e-06


CHUNKS = 4


def from_behind(value, axis, steps):
    count = lax.axis_size(axis)
    pairs = [(source, (source + steps) % count) for source in range(count)]
    return lax.ppermute(value, axis, pairs)


def hand_over(value, steps):
    sections, count = lax.axis_size("section"), lax.axis_size("kv")
    pairs = [
        (s * count + k, ((s + 1) % sections) * count + (k + steps) % count)
        for s in range(sections)
        for k in range(count)
    ]
    return lax.ppermute(value, ("section", "kv"), pairs)


def after(value, *earlier):
    return lax.optimization_barrier((value, *earlier))[0]


def gather_features(block, earlier):
    if lax.axis_size("tp") != 2:
        return lax.all_gather(block, "tp", axis=1, tiled=True)
    other = from_behind(block, "tp", 1)
    if earlier is not None:
        other = after(other, earlier)
    first = lax.axis_index("tp") == 0
    return jnp.concatenate(
        [jnp.where(first, block, other), jnp.where(first, other, block)], axis=1
    )


def sum_over_tp(value):
    if lax.axis_size("tp") != 2:
        return lax.psum(value, "tp")
    return value + from_behind(value, "tp", 1)


def columns_of(w_kv, member):
    width = w_kv.shape[2] // lax.axis_size("tp")
    part = lax.dynamic_slice_in_dim(w_kv, member * width, width, axis=2)
    return part.reshape(w_kv.shape[0], 2 * width)


def block_ranks(owners):
    per_block = owners.shape[1]
    same_owner = owners[:, :, None] == owners[:, None, :]
    earlier = jnp.arange(per_block)[None, :] < jnp.arange(per_block)[:, None]
    return jnp.sum((same_owner & earlier[None, :, :]).astype(jnp.int32), axis=2)


def attend_kernel(head_count, parts, query_ref, *refs):
    masks, stores = refs[:parts], refs[parts : 2 * parts]
    totals_ref, weighted_ref = refs[2 * parts :]
    half = head_count * HEAD_DIM
    for k in range(head_count):
        query = query_ref[k]
        total = jnp.zeros((query.shape[0], 1), jnp.float32)
        numer = jnp.zeros((query.shape[0], HEAD_DIM), jnp.float32)
        for mask_ref, store_ref in zip(masks, stores):
            keys = store_ref[:, k * HEAD_DIM : (k + 1) * HEAD_DIM]
            values = store_ref[:, half + k * HEAD_DIM : half + (k + 1) * HEAD_DIM]
            raw = lax.dot_general(
                query, keys, (((1,), (1,)), ((), ())), preferred_element_type=jnp.float32
            )
            capped = softcap * jnp.tanh(raw * query_scale / softcap)
            weights = jnp.where(mask_ref[...] > 0.0, jnp.exp(capped), jnp.float32(0.0))
            total = total + jnp.sum(weights, axis=1, keepdims=True)
            numer = numer + jnp.dot(
                weights.astype(jnp.bfloat16), values, preferred_element_type=jnp.float32
            )
        totals_ref[k] = jnp.broadcast_to(total, numer.shape)
        weighted_ref[k] = numer


def attend_all(query_grid, masks, stores):
    head_count, rows = query_grid.shape[:2]
    tokens = sum(store.shape[0] for store in stores)
    result = jax.ShapeDtypeStruct((head_count, rows, HEAD_DIM), jnp.float32)
    return pl.pallas_call(
        lambda *refs: attend_kernel(head_count, len(stores), *refs),
        out_shape=(result, result),
        in_specs=[pl.BlockSpec(memory_space=pltpu.VMEM)] * (1 + 2 * len(stores)),
        out_specs=(pl.BlockSpec(memory_space=pltpu.VMEM),) * 2,
        compiler_params=pltpu.CompilerParams(vmem_limit_bytes=40 * 1024 * 1024),
        cost_estimate=pl.CostEstimate(
            flops=4 * tokens * head_count * rows * HEAD_DIM * 8,
            bytes_accessed=4 * tokens * head_count * HEAD_DIM,
            transcendentals=2 * tokens * head_count * rows,
        ),
    )(query_grid, *masks, *stores)


def sum_over_kv(value):
    count = lax.axis_size("kv")
    if count > 4:
        return lax.psum(value, "kv")
    here = lax.axis_index("kv")
    shifted = jnp.stack([from_behind(value, "kv", j) if j else value for j in range(count)])
    total = jnp.zeros_like(value)
    for source in range(count):
        total = total + lax.dynamic_index_in_dim(
            shifted, (here - source + count) % count, 0, keepdims=False
        )
    return total


def per_device(
    patches,
    vis_gain,
    vis_bias,
    w_proj,
    b_proj,
    rms_gain,
    w_kv,
    queries,
    cache,
    cache_lengths,
    slot_page,
    page_owner,
    image_request,
):
    kv_count = lax.axis_size("kv")
    section_count = lax.axis_size("section")
    section_idx = lax.axis_index("section")
    kv_idx = lax.axis_index("kv")
    row_count = patches.shape[0]
    page_len = cache.shape[1]
    pages_dev = row_count // page_len
    capacity = max(2, (2 * pages_dev + kv_count - 1) // kv_count)
    recv_slots = kv_count * capacity
    tp_count = lax.axis_size("tp")
    tp_idx = lax.axis_index("tp")
    full_w = lax.all_gather(w_proj, "section", axis=0, tiled=True)
    full_width = w_proj.shape[1] * tp_count
    w_parts = [columns_of(w_kv, (tp_idx + j) % tp_count) for j in range(tp_count)]
    tokens = page_len // CHUNKS
    patch_pages = patches.reshape(pages_dev, page_len, -1)
    next_group = (section_idx + 1) % section_count
    next_owners = lax.dynamic_index_in_dim(page_owner, next_group, 0, keepdims=False).reshape(
        kv_count, pages_dev
    )
    my_owner = lax.dynamic_index_in_dim(next_owners, kv_idx, 0, keepdims=False)
    my_rank = lax.dynamic_index_in_dim(block_ranks(next_owners), kv_idx, 0, keepdims=False)
    new_pages = jnp.zeros((recv_slots, page_len, 2, cache.shape[3]), jnp.bfloat16)
    encoded_parts = []
    sent_before, encoded_before, marker = None, None, []
    last = kv_count // 2
    shifts = [j for j in range(1, kv_count) if j != last] + [0, last]
    waiting = []

    def write_pages(pages, blocks):
        for block, slot, token in blocks:
            pages = lax.dynamic_update_slice(
                pages, block.reshape(capacity, tokens, 2, -1), (slot, token, 0, 0)
            )
        return pages

    for c in range(CHUNKS):
        block = patch_pages[:, c * tokens : (c + 1) * tokens, :].reshape(pages_dev * tokens, -1)
        gathered = gather_features(block, sent_before).astype(jnp.float32)
        row_mean = jnp.mean(gathered, axis=1, keepdims=True)
        centred = gathered - row_mean
        variance = jnp.mean(centred * centred, axis=1, keepdims=True)
        x_norm = (centred * lax.rsqrt(variance + epsilon) * vis_gain + vis_bias).astype(
            jnp.bfloat16
        )
        projected = jnp.dot(x_norm, full_w, preferred_element_type=jnp.float32) + b_proj
        squares_before = jnp.sum(projected * projected, axis=1)
        squares = sum_over_tp(squares_before)
        hidden = (
            projected * lax.rsqrt(squares / full_width + epsilon)[:, None] * rms_gain
        ).astype(jnp.bfloat16)
        if encoded_before is not None:
            hidden = after(hidden, encoded_before)
        sent = [
            jnp.dot(hidden, w_parts[j], preferred_element_type=jnp.float32).astype(jnp.bfloat16)
            for j in range(1, tp_count)
        ]
        arrived = [from_behind(part, "tp", j + 1) for j, part in enumerate(sent)]
        sent_before = sent[0] if c == 0 else squares_before
        hidden = after(hidden, *marker)
        marker = []
        image_kv = jnp.dot(hidden, w_parts[0], preferred_element_type=jnp.float32)
        for part in arrived:
            image_kv = image_kv + part.astype(jnp.float32)
        encoded = image_kv.astype(jnp.bfloat16).reshape(pages_dev, tokens, -1)
        encoded_before = encoded
        encoded_parts.append(encoded)
        for j in shifts:
            owner = (kv_idx + j) % kv_count
            placing = (
                (jnp.arange(capacity)[:, None] == my_rank[None, :]) & (my_owner == owner)[None, :]
            ).astype(jnp.bfloat16)
            outgoing = jnp.einsum(
                "jp,ptf->jtf", placing, encoded, preferred_element_type=jnp.float32
            ).astype(jnp.bfloat16)
            if j == shifts[0]:
                waiting = [(after(block, outgoing), *place) for block, *place in waiting]
                new_pages = write_pages(new_pages, waiting)
                waiting = []
            incoming = hand_over(outgoing, j)
            source = (kv_idx - j + kv_count) % kv_count
            if j != last:
                marker.append(incoming)
                new_pages = write_pages(new_pages, [(incoming, source * capacity, c * tokens)])
            else:
                waiting.append((incoming, source * capacity, c * tokens))
    next_queries = from_behind(queries, "section", section_count - 1)
    next_request = from_behind(image_request, "section", section_count - 1)
    cache = after(cache, marker[0])
    next_queries = after(next_queries, marker[0])
    req_count = queries.shape[0]
    kv_heads_dev = cache.shape[3] // HEAD_DIM
    group_size = queries.shape[1] // HEAD_DIM // kv_heads_dev

    def grid_of(rows):
        return (
            rows.reshape(req_count, kv_heads_dev, group_size, HEAD_DIM)
            .transpose(1, 0, 2, 3)
            .reshape(kv_heads_dev, req_count * group_size, HEAD_DIM)
        )

    lengths = cache_lengths[0]
    page_counts = (lengths + page_len - 1) // page_len
    starts = jnp.cumsum(page_counts) - page_counts
    slot_ids = slot_page[0]
    within = slot_ids[:, None] - starts[None, :]
    inside = (within >= 0) & (within < page_counts[None, :])
    valid = jnp.where(inside, jnp.clip(lengths[None, :] - within * page_len, 0, page_len), 0)
    cache_mask = jnp.arange(page_len)[None, :, None] < valid[:, None, :]
    image_of = (kv_idx * pages_dev + jnp.arange(pages_dev)) // IMAGE_PAGES
    image_hit = image_of[:, None] == jnp.arange(next_request.shape[1])[None, :]
    page_request = jnp.sum(jnp.where(image_hit, next_request[0][None, :], 0), axis=1)
    request_hit = page_request[:, None] == jnp.arange(req_count)[None, :]
    handed_mask = jnp.broadcast_to(request_hit[:, None, :], (pages_dev, tokens, req_count))

    def grouped(mask):
        rows = mask.reshape(-1, req_count).T.astype(jnp.float32)
        return jnp.repeat(rows, group_size, axis=0)

    image_sums = attend_all(
        grid_of(next_queries),
        [grouped(handed_mask)] * CHUNKS,
        [encoded.reshape(pages_dev * tokens, -1) for encoded in encoded_parts],
    )
    cache_sums = attend_all(
        grid_of(queries), [grouped(cache_mask)], [cache.reshape(-1, 2 * cache.shape[3])]
    )
    handed_sums = from_behind(jnp.stack(image_sums), "section", 1)
    local_sums = jnp.stack(cache_sums) + handed_sums
    waiting = [(after(block, local_sums), *place) for block, *place in waiting]
    new_pages = write_pages(new_pages, waiting)
    totals, weighted = sum_over_kv(local_sums)
    attended = (
        (weighted / totals)
        .astype(jnp.bfloat16)
        .reshape(kv_heads_dev, req_count, group_size, HEAD_DIM)
        .transpose(1, 0, 2, 3)
        .reshape(req_count, -1)
    )
    return (new_pages, attended)


def solution(mesh):
    in_specs = (
        P(("section", "kv"), "tp"),
        P(),
        P(),
        P("section", "tp"),
        P("tp"),
        P("tp"),
        P("tp", None, None),
        P("section", "tp"),
        P(("section", "kv"), None, None, "tp"),
        P("section", None),
        P("section", "kv"),
        P(),
        P("section", None),
    )
    out_specs = (P(("section", "kv"), None, None, "tp"), P("section", "tp"))
    return jax.shard_map(
        per_device, mesh=mesh, in_specs=in_specs, out_specs=out_specs, check_vma=False
    )
```

```python
import jax
import jax.numpy as jnp
from jax import lax
from jax.experimental import pallas as pl
from jax.experimental.pallas import tpu as pltpu
from jax.sharding import PartitionSpec as P

HEAD_DIM = 128
IMAGE_PAGES = 32


query_scale = 1.0 / 12.0
softcap = 50.0
epsilon = 1e-06


CHUNKS = 4


def from_behind(value, axis, steps):
    count = lax.axis_size(axis)
    pairs = [(source, (source + steps) % count) for source in range(count)]
    return lax.ppermute(value, axis, pairs)


def hand_over(value, steps):
    sections, count = lax.axis_size("section"), lax.axis_size("kv")
    pairs = [
        (s * count + k, ((s + 1) % sections) * count + (k + steps) % count)
        for s in range(sections)
        for k in range(count)
    ]
    return lax.ppermute(value, ("section", "kv"), pairs)


def after(value, *earlier):
    return lax.optimization_barrier((value, *earlier))[0]


def gather_features(block, earlier):
    if lax.axis_size("tp") != 2:
        return lax.all_gather(block, "tp", axis=1, tiled=True)
    other = from_behind(block, "tp", 1)
    if earlier is not None:
        other = after(other, earlier)
    first = lax.axis_index("tp") == 0
    return jnp.concatenate(
        [jnp.where(first, block, other), jnp.where(first, other, block)], axis=1
    )


def sum_over_tp(value):
    if lax.axis_size("tp") != 2:
        return lax.psum(value, "tp")
    return value + from_behind(value, "tp", 1)


def columns_of(w_kv, member):
    width = w_kv.shape[2] // lax.axis_size("tp")
    part = lax.dynamic_slice_in_dim(w_kv, member * width, width, axis=2)
    return part.reshape(w_kv.shape[0], 2 * width)


def block_ranks(owners):
    per_block = owners.shape[1]
    same_owner = owners[:, :, None] == owners[:, None, :]
    earlier = jnp.arange(per_block)[None, :] < jnp.arange(per_block)[:, None]
    return jnp.sum((same_owner & earlier[None, :, :]).astype(jnp.int32), axis=2)


def attend_kernel(head_count, parts, query_ref, *refs):
    masks, stores = refs[:parts], refs[parts : 2 * parts]
    totals_ref, weighted_ref = refs[2 * parts :]
    half = head_count * HEAD_DIM
    for k in range(head_count):
        query = query_ref[k]
        total = jnp.zeros((query.shape[0], 1), jnp.float32)
        numer = jnp.zeros((query.shape[0], HEAD_DIM), jnp.float32)
        for mask_ref, store_ref in zip(masks, stores):
            keys = store_ref[:, k * HEAD_DIM : (k + 1) * HEAD_DIM]
            values = store_ref[:, half + k * HEAD_DIM : half + (k + 1) * HEAD_DIM]
            raw = lax.dot_general(
                query, keys, (((1,), (1,)), ((), ())), preferred_element_type=jnp.float32
            )
            capped = softcap * jnp.tanh(raw * query_scale / softcap)
            weights = jnp.where(mask_ref[...] > 0.0, jnp.exp(capped), jnp.float32(0.0))
            total = total + jnp.sum(weights, axis=1, keepdims=True)
            numer = numer + jnp.dot(
                weights.astype(jnp.bfloat16), values, preferred_element_type=jnp.float32
            )
        totals_ref[k] = jnp.broadcast_to(total, numer.shape)
        weighted_ref[k] = numer


def attend_all(query_grid, masks, stores):
    head_count, rows = query_grid.shape[:2]
    tokens = sum(store.shape[0] for store in stores)
    result = jax.ShapeDtypeStruct((head_count, rows, HEAD_DIM), jnp.float32)
    return pl.pallas_call(
        lambda *refs: attend_kernel(head_count, len(stores), *refs),
        out_shape=(result, result),
        in_specs=[pl.BlockSpec(memory_space=pltpu.VMEM)] * (1 + 2 * len(stores)),
        out_specs=(pl.BlockSpec(memory_space=pltpu.VMEM),) * 2,
        compiler_params=pltpu.CompilerParams(vmem_limit_bytes=40 * 1024 * 1024),
        cost_estimate=pl.CostEstimate(
            flops=4 * tokens * head_count * rows * HEAD_DIM * 8,
            bytes_accessed=4 * tokens * head_count * HEAD_DIM,
            transcendentals=2 * tokens * head_count * rows,
        ),
    )(query_grid, *masks, *stores)


def sum_over_kv(value):
    count = lax.axis_size("kv")
    if count > 4:
        return lax.psum(value, "kv")
    here = lax.axis_index("kv")
    shifted = jnp.stack([from_behind(value, "kv", j) if j else value for j in range(count)])
    total = jnp.zeros_like(value)
    for source in range(count):
        total = total + lax.dynamic_index_in_dim(
            shifted, (here - source + count) % count, 0, keepdims=False
        )
    return total


def per_device(
    patches,
    vis_gain,
    vis_bias,
    w_proj,
    b_proj,
    rms_gain,
    w_kv,
    queries,
    cache,
    cache_lengths,
    slot_page,
    page_owner,
    image_request,
):
    kv_count = lax.axis_size("kv")
    section_count = lax.axis_size("section")
    section_idx = lax.axis_index("section")
    kv_idx = lax.axis_index("kv")
    row_count = patches.shape[0]
    page_len = cache.shape[1]
    pages_dev = row_count // page_len
    capacity = max(2, (2 * pages_dev + kv_count - 1) // kv_count)
    recv_slots = kv_count * capacity
    tp_count = lax.axis_size("tp")
    tp_idx = lax.axis_index("tp")
    full_w = lax.all_gather(w_proj, "section", axis=0, tiled=True)
    full_width = w_proj.shape[1] * tp_count
    w_parts = [columns_of(w_kv, (tp_idx + j) % tp_count) for j in range(tp_count)]
    tokens = page_len // CHUNKS
    patch_pages = patches.reshape(pages_dev, page_len, -1)
    next_group = (section_idx + 1) % section_count
    next_owners = lax.dynamic_index_in_dim(page_owner, next_group, 0, keepdims=False).reshape(
        kv_count, pages_dev
    )
    my_owner = lax.dynamic_index_in_dim(next_owners, kv_idx, 0, keepdims=False)
    my_rank = lax.dynamic_index_in_dim(block_ranks(next_owners), kv_idx, 0, keepdims=False)
    new_pages = jnp.zeros((recv_slots, page_len, 2, cache.shape[3]), jnp.bfloat16)
    encoded_parts = []
    sent_before, encoded_before, marker = None, None, []
    last = kv_count // 2
    shifts = [j for j in range(1, kv_count) if j != last] + [0, last]
    waiting = []

    def write_pages(pages, blocks):
        for block, slot, token in blocks:
            pages = lax.dynamic_update_slice(
                pages, block.reshape(capacity, tokens, 2, -1), (slot, token, 0, 0)
            )
        return pages

    for c in range(CHUNKS):
        block = patch_pages[:, c * tokens : (c + 1) * tokens, :].reshape(pages_dev * tokens, -1)
        gathered = gather_features(block, sent_before).astype(jnp.float32)
        row_mean = jnp.mean(gathered, axis=1, keepdims=True)
        centred = gathered - row_mean
        variance = jnp.mean(centred * centred, axis=1, keepdims=True)
        x_norm = (centred * lax.rsqrt(variance + epsilon) * vis_gain + vis_bias).astype(
            jnp.bfloat16
        )
        projected = jnp.dot(x_norm, full_w, preferred_element_type=jnp.float32) + b_proj
        squares_before = jnp.sum(projected * projected, axis=1)
        squares = sum_over_tp(squares_before)
        hidden = (
            projected * lax.rsqrt(squares / full_width + epsilon)[:, None] * rms_gain
        ).astype(jnp.bfloat16)
        if encoded_before is not None:
            hidden = after(hidden, encoded_before)
        sent = [
            jnp.dot(hidden, w_parts[j], preferred_element_type=jnp.float32).astype(jnp.bfloat16)
            for j in range(1, tp_count)
        ]
        arrived = [from_behind(part, "tp", j + 1) for j, part in enumerate(sent)]
        sent_before = sent[0] if c == 0 else encoded_parts[0] if c == 1 else squares_before
        hidden = after(hidden, *marker)
        marker = []
        image_kv = jnp.dot(hidden, w_parts[0], preferred_element_type=jnp.float32)
        for part in arrived:
            image_kv = image_kv + part.astype(jnp.float32)
        encoded = image_kv.astype(jnp.bfloat16).reshape(pages_dev, tokens, -1)
        encoded_before = encoded
        encoded_parts.append(encoded)
        for j in shifts:
            owner = (kv_idx + j) % kv_count
            placing = (
                (jnp.arange(capacity)[:, None] == my_rank[None, :]) & (my_owner == owner)[None, :]
            ).astype(jnp.bfloat16)
            outgoing = jnp.einsum(
                "jp,ptf->jtf", placing, encoded, preferred_element_type=jnp.float32
            ).astype(jnp.bfloat16)
            if j == shifts[0]:
                waiting = [(after(block, outgoing), *place) for block, *place in waiting]
                new_pages = write_pages(new_pages, waiting)
                waiting = []
            incoming = hand_over(outgoing, j)
            source = (kv_idx - j + kv_count) % kv_count
            if j != last:
                marker.append(incoming)
                new_pages = write_pages(new_pages, [(incoming, source * capacity, c * tokens)])
            else:
                waiting.append((incoming, source * capacity, c * tokens))
    next_queries = from_behind(queries, "section", section_count - 1)
    next_request = from_behind(image_request, "section", section_count - 1)
    cache = after(cache, marker[0])
    next_queries = after(next_queries, marker[0])
    req_count = queries.shape[0]
    kv_heads_dev = cache.shape[3] // HEAD_DIM
    group_size = queries.shape[1] // HEAD_DIM // kv_heads_dev

    def grid_of(rows):
        return (
            rows.reshape(req_count, kv_heads_dev, group_size, HEAD_DIM)
            .transpose(1, 0, 2, 3)
            .reshape(kv_heads_dev, req_count * group_size, HEAD_DIM)
        )

    lengths = cache_lengths[0]
    page_counts = (lengths + page_len - 1) // page_len
    starts = jnp.cumsum(page_counts) - page_counts
    slot_ids = slot_page[0]
    within = slot_ids[:, None] - starts[None, :]
    inside = (within >= 0) & (within < page_counts[None, :])
    valid = jnp.where(inside, jnp.clip(lengths[None, :] - within * page_len, 0, page_len), 0)
    cache_mask = jnp.arange(page_len)[None, :, None] < valid[:, None, :]
    image_of = (kv_idx * pages_dev + jnp.arange(pages_dev)) // IMAGE_PAGES
    image_hit = image_of[:, None] == jnp.arange(next_request.shape[1])[None, :]
    page_request = jnp.sum(jnp.where(image_hit, next_request[0][None, :], 0), axis=1)
    request_hit = page_request[:, None] == jnp.arange(req_count)[None, :]
    handed_mask = jnp.broadcast_to(request_hit[:, None, :], (pages_dev, tokens, req_count))

    def grouped(mask):
        rows = mask.reshape(-1, req_count).T.astype(jnp.float32)
        return jnp.repeat(rows, group_size, axis=0)

    image_sums = attend_all(
        grid_of(next_queries),
        [grouped(handed_mask)] * CHUNKS,
        [encoded.reshape(pages_dev * tokens, -1) for encoded in encoded_parts],
    )
    cache_sums = attend_all(
        grid_of(queries), [grouped(cache_mask)], [cache.reshape(-1, 2 * cache.shape[3])]
    )
    handed_sums = from_behind(jnp.stack(image_sums), "section", 1)
    local_sums = jnp.stack(cache_sums) + handed_sums
    waiting = [(after(block, local_sums), *place) for block, *place in waiting]
    new_pages = write_pages(new_pages, waiting)
    totals, weighted = sum_over_kv(local_sums)
    attended = (
        (weighted / totals)
        .astype(jnp.bfloat16)
        .reshape(kv_heads_dev, req_count, group_size, HEAD_DIM)
        .transpose(1, 0, 2, 3)
        .reshape(req_count, -1)
    )
    return (new_pages, attended)


def solution(mesh):
    in_specs = (
        P(("section", "kv"), "tp"),
        P(),
        P(),
        P("section", "tp"),
        P("tp"),
        P("tp"),
        P("tp", None, None),
        P("section", "tp"),
        P(("section", "kv"), None, None, "tp"),
        P("section", None),
        P("section", "kv"),
        P(),
        P("section", None),
    )
    out_specs = (P(("section", "kv"), None, None, "tp"), P("section", "tp"))
    return jax.shard_map(
        per_device, mesh=mesh, in_specs=in_specs, out_specs=out_specs, check_vma=False
    )
```
